32 devices in a mesh: batch: 8 (over y, x, core), patch: 4 (over z).
Axes of the slice: x: 2, y: 2, z: 4, core: 2. Of those that a mesh axis runs over, the one named last changes fastest.
Arguments:
- hidden_in: bfloat16 [12288, 1280], P(('batch', 'patch')), parts along dimension 0, may hold values from -45 to 45
- stale_keys: bfloat16 [12288, 1280], P(('batch', 'patch')), parts along dimension 0, may hold values from -150 to 150
- stale_values: bfloat16 [12288, 1280], P(('batch', 'patch')), parts along dimension 0, may hold values from -12 to 12
- stale_moments: float32 [192, 2, 2, 32], P(('batch', 'patch')), parts along dimension 0, may hold values from -5120 to 102400, as said below
- gain_attn: float32 [1280], replicated, may hold values from 0.1 to 1.9
- bias_attn: float32 [1280], replicated, may hold values from -3 to 3
- w_query: bfloat16 [1280, 1280], replicated, may hold values from -0.3125 to 0.3125
- w_key: bfloat16 [1280, 1280], replicated, may hold values from -0.625 to 0.625
- w_value: bfloat16 [1280, 1280], replicated, may hold values from -0.625 to 0.625
- gain_conv: float32 [1280], replicated, may hold values from 0.1 to 1.9
- bias_conv: float32 [1280], replicated, may hold values from -3 to 3
- conv_weight: bfloat16 [3, 3, 1280, 640], replicated, may hold values from -0.0546875 to 0.0546875
- conv_bias: float32 [640], replicated, may hold values from -3 to 3
- w_time: bfloat16 [320, 640], replicated, may hold values from -0.3125 to 0.3125
- timestep: int32 [1], replicated, may hold values from 0 to 999
Outputs:
- conv_out: bfloat16 [12288, 640], P(('batch', 'patch')), parts along dimension 0
The draws below stay inside these ranges and needn't reach their ends.
There are 8 independent parts, one for each index of `batch`. The reference program is written for one: setup_inputs(seed, part) draws one part's arguments, and reference() takes and returns one part's arrays. A program takes and returns all parts, laid end to end along the dimension named above; an argument that names none is the same for every part. Nothing has to cross between parts.
Inputs may be any that keep to these rules, and one draw needn't show every extreme that they name: `stale_moments`: each row's entries are the sums and sums of squares of 2560 values: that count times the second is at least the square of the first.
All inputs are finite; a program needn't handle non-finite values.
Results may differ from the reference program's by a relative error of at most 0.008.
The reference program's roundings to bfloat16 on the way count: a program that leaves them out, or rounds other values in their place, can miss the bound.
Values may be sent and summed in bfloat16 or wider, within the bound.
A program may use at most 320 MiB of HBM per device.

```python
import math
import jax
import jax.numpy as jnp
from jax import lax

HEADS = 20
HEAD_DIM = 64
GROUPS = 32
TDIM = 320
COUT = 640
W = 64
ROWS_DEV = 6
C = 1280
TOK_DEV = 384
NROWS = 24
NTOK = 1536
N_PATCH = 4


def draw_hidden_in(key, part):
    key_one, key_two, key_three = jax.random.split(key, 3)
    row_scale = jnp.exp(jax.random.uniform(key_two, (NTOK, 1), minval=math.log(0.5), maxval=math.log(3.0)))
    chan_scale = jnp.exp(jax.random.uniform(key_three, (1, C), minval=math.log(0.5), maxval=math.log(3.0)))
    sampled = jnp.clip(jax.random.normal(key_one, (NTOK, C)), -5.0, 5.0) * row_scale
    return (sampled * chan_scale).astype(jnp.bfloat16)


def stale_pair(key):
    base_key = jax.random.fold_in(key, 17)
    key_one = jax.random.fold_in(base_key, 0)
    key_four = jax.random.fold_in(base_key, 3)
    sampled = 4.0 * jnp.clip(jax.random.normal(key_one, (NTOK, C)), -5.0, 5.0)
    noise = jnp.clip(jax.random.normal(key_four, (NTOK, C)), -5.0, 5.0)
    keys_drawn = sampled.astype(jnp.bfloat16)
    values_drawn = jnp.clip(0.5 * sampled + noise, -12.0, 12.0).astype(jnp.bfloat16)
    return (keys_drawn, values_drawn)


def draw_stale_keys(key, part):
    return stale_pair(key)[0]


def draw_stale_values(key, part):
    return stale_pair(key)[1]


def draw_stale_moments(key, part):
    key_one, key_two = jax.random.split(key, 2)
    cells = W * (C // GROUPS)
    positions = jnp.arange(NROWS, dtype=jnp.float32) / max(NROWS - 1, 1)
    rising = (10.0 ** positions)[:, None, None]
    variance = rising * jnp.exp(jax.random.uniform(key_one, (NROWS, 2, GROUPS), minval=math.log(0.5), maxval=math.log(2.0)))
    average = jnp.clip(jax.random.normal(key_two, (NROWS, 2, GROUPS)), -2.0, 2.0)
    first_sum = cells * average
    second_sum = cells * (variance + average * average)
    return jnp.stack([first_sum, second_sum], axis=2).astype(jnp.float32)


def bell_draw(rng, extent, width, bound, held_as=jnp.bfloat16):
    return jnp.clip(width * jax.random.normal(rng, extent, jnp.float32), -bound, bound).astype(held_as)


def setup_inputs(seed: int = 0, part: int = 0) -> dict:
    key_list = jax.random.split(jax.random.key(seed), 16)
    own_keys = jax.random.split(jax.random.fold_in(key_list[15], part), 16)
    return {
        "hidden_in": draw_hidden_in(jax.random.fold_in(jax.random.fold_in(key_list[15], part), 71), part),
        "stale_keys": draw_stale_keys(jax.random.fold_in(jax.random.fold_in(key_list[15], part), 71), part),
        "stale_values": draw_stale_values(jax.random.fold_in(jax.random.fold_in(key_list[15], part), 71), part),
        "stale_moments": draw_stale_moments(jax.random.fold_in(jax.random.fold_in(key_list[15], part), 71), part),
        "gain_attn": jnp.clip(1.0 + 0.18 * jax.random.normal(key_list[4], (C,), jnp.float32), 0.1, 1.9),
        "bias_attn": bell_draw(key_list[5], (C,), 0.5, 3.0, jnp.float32),
        "w_query": bell_draw(key_list[6], (C, C), (C // 4) ** -0.5, 0.3125),
        "w_key": bell_draw(key_list[7], (C, C), (C // 16) ** -0.5, 0.625),
        "w_value": bell_draw(key_list[8], (C, C), (C // 16) ** -0.5, 0.625),
        "gain_conv": jnp.clip(1.0 + 0.18 * jax.random.normal(key_list[9], (C,), jnp.float32), 0.1, 1.9),
        "bias_conv": bell_draw(key_list[10], (C,), 0.5, 3.0, jnp.float32),
        "conv_weight": bell_draw(key_list[11], (3, 3, C, COUT), (9 * C) ** -0.5, 0.0546875),
        "conv_bias": bell_draw(key_list[12], (COUT,), 0.5, 3.0, jnp.float32),
        "w_time": bell_draw(key_list[13], (TDIM, COUT), TDIM ** -0.5, 0.3125),
        "timestep": jax.random.randint(key_list[14], (1,), 0, 1000).astype(jnp.int32),
    }


EPS = 1e-05

def group_moments(rows_in, groups):
    values = rows_in.astype(jnp.float32).reshape(rows_in.shape[0], groups, rows_in.shape[1] // groups)
    return jnp.stack([lax.optimization_barrier(jnp.sum(values, axis=(0, 2))), lax.optimization_barrier(jnp.sum(values * values, axis=(0, 2)))])

def group_normalize(rows_in, totals, count, gain, offset, groups):
    average = totals[0] / count
    variance = totals[1] / count - average * average
    inverse = lax.rsqrt(variance + EPS)
    group_width = rows_in.shape[1] // groups
    factors = jnp.repeat(inverse, group_width) * gain
    shifts = offset - jnp.repeat(average * inverse, group_width) * gain
    return rows_in.astype(jnp.float32) * factors + shifts

def time_embedding(timestep, w_time):
    half_dim = w_time.shape[0] // 2
    frequency = jnp.exp(-math.log(10000.0) * jnp.arange(half_dim, dtype=jnp.float32) / half_dim)
    angles = timestep[0].astype(jnp.float32) * frequency
    embedded = jnp.concatenate([jnp.cos(angles), jnp.sin(angles)])
    return jnp.dot(embedded[None, :], w_time.astype(jnp.float32), precision=lax.Precision.HIGHEST)[0]

def reference(hidden_in, stale_keys, stale_values, stale_moments, gain_attn, bias_attn, w_query, w_key, w_value, gain_conv, bias_conv, conv_weight, conv_bias, w_time, timestep):
    count = NTOK * (C // GROUPS)
    stale_total = lax.optimization_barrier(jnp.sum(stale_moments, axis=0))
    scale_qk = HEAD_DIM ** (-0.5)

    def strip_result(strip):
        first_tok = (strip * TOK_DEV).astype(jnp.int32)
        first_row = (strip * ROWS_DEV).astype(jnp.int32)
        rows_in = lax.dynamic_slice_in_dim(hidden_in, first_tok, TOK_DEV, 0)
        stale_strip = lax.optimization_barrier(jnp.sum(lax.dynamic_slice_in_dim(stale_moments, first_row, ROWS_DEV, 0), axis=0))
        totals_attn = stale_total[0] - stale_strip[0] + group_moments(rows_in, GROUPS)
        normed = group_normalize(rows_in, totals_attn, count, gain_attn, bias_attn, GROUPS).astype(jnp.bfloat16)
        query = jnp.dot(normed, w_query, preferred_element_type=jnp.float32).astype(jnp.bfloat16)
        key_fresh = jnp.dot(normed, w_key, preferred_element_type=jnp.float32).astype(jnp.bfloat16)
        value_fresh = jnp.dot(normed, w_value, preferred_element_type=jnp.float32).astype(jnp.bfloat16)
        keys_used = lax.dynamic_update_slice_in_dim(stale_keys, key_fresh, first_tok, 0)
        values_used = lax.dynamic_update_slice_in_dim(stale_values, value_fresh, first_tok, 0)
        query3 = query.astype(jnp.float32).reshape(TOK_DEV, HEADS, HEAD_DIM)
        keys3 = keys_used.astype(jnp.float32).reshape(NTOK, HEADS, HEAD_DIM)
        values3 = values_used.astype(jnp.float32).reshape(NTOK, HEADS, HEAD_DIM)
        scores = jnp.einsum('qhd,khd->qhk', query3, keys3) * scale_qk
        row_max = lax.optimization_barrier(jnp.max(scores, axis=-1, keepdims=True))
        weights = jnp.exp(scores - row_max)
        row_total = lax.optimization_barrier(jnp.sum(weights, axis=-1))
        probs = weights.astype(jnp.bfloat16).astype(jnp.float32)
        weighted = jnp.einsum('qhk,khd->qhd', probs, values3)
        attended = (weighted / row_total[..., None]).reshape(TOK_DEV, C)
        updated = (rows_in.astype(jnp.float32) + attended).astype(jnp.bfloat16)
        totals_conv = stale_total[1] - stale_strip[1] + group_moments(updated, GROUPS)
        normed_conv = group_normalize(updated, totals_conv, count, gain_conv, bias_conv, GROUPS)
        return jax.nn.silu(normed_conv).astype(jnp.bfloat16)
    strips = lax.map(strip_result, jnp.arange(N_PATCH, dtype=jnp.int32))
    latent_grid = strips.reshape(1, NROWS, W, C)
    convolved = lax.conv_general_dilated(latent_grid, conv_weight, (1, 1), ((1, 1), (1, 1)), dimension_numbers=('NHWC', 'HWIO', 'NHWC'), preferred_element_type=jnp.float32)[0]
    temb = time_embedding(timestep, w_time)
    conv_out = (convolved + conv_bias + temb).astype(jnp.bfloat16)
    return conv_out.reshape(NTOK, COUT)
```

```python
import functools
import math

import jax
import jax.numpy as jnp
from jax import lax
from jax.experimental import pallas as pl
from jax.experimental.pallas import tpu as pltpu
from jax.sharding import PartitionSpec as P

HEADS = 20
GROUPS = 32
W = 64
EPS = 1e-05
PW = 128
AHEAD = 2
F32 = jnp.float32
BF16 = jnp.bfloat16
HI = lax.Precision.HIGHEST


def is_lent(n, p):
    if n < 4:
        return p < 0
    return (lax.rem(p, 2) == 0) & (p >= 2)


def lent_index(p):
    return jnp.maximum(lax.div(p, 2) - 1, 0)


def kernel(
    n,
    hidden_hbm,
    keys_hbm,
    values_hbm,
    moments_ref,
    gain_a,
    bias_a,
    gain_c,
    bias_c,
    wqkv_q,
    wqkv_k,
    wqkv_v,
    wconv_hbm,
    bias_out,
    out_ref,
    hid,
    wq,
    wconv,
    kv,
    q_ref,
    q_in,
    lent_out,
    lent_in,
    stat_out,
    stat_in,
    sbuf,
    ot,
    upd,
    act,
    ybuf,
    sums,
    rows_n,
    mom,
    local_sem,
    send_r,
    send_l,
    recv,
    mom_send,
    mom_recv,
    lend_send,
    lend_recv,
    halo_send,
    halo_recv,
):
    me = lax.axis_index("patch")
    tok, chan = hid.shape
    pairs = chan // PW
    count = n * tok * (chan // GROUPS)
    last = n - 1
    has_left, has_right = me > 0, me < last
    is_end = (me == 0) | (me == last)
    is_server = ((me == 1) | (me == n - 2)) if n >= 4 else (me < 0)
    served = jnp.where(me == 1, 0, last)
    server = jnp.where(me == 0, 1, last - 1)

    def remote(src, dst, ssem, rsem, to):
        return pltpu.make_async_remote_copy(
            src_ref=src,
            dst_ref=dst,
            send_sem=ssem,
            recv_sem=rsem,
            device_id={"patch": to},
            device_id_type=pl.DeviceIdType.MESH,
        )

    barrier = pltpu.get_barrier_semaphore()

    @pl.when(has_left)
    def _():
        pl.semaphore_signal(
            barrier, inc=1, device_id={"patch": me - 1}, device_id_type=pl.DeviceIdType.MESH
        )

    @pl.when(has_right)
    def _():
        pl.semaphore_signal(
            barrier, inc=1, device_id={"patch": me + 1}, device_id_type=pl.DeviceIdType.MESH
        )

    load_hid = pltpu.make_async_copy(hidden_hbm, hid, local_sem.at[0])
    load_hid.start()
    load_w = [
        pltpu.make_async_copy(w, wq.at[i], local_sem.at[1 + i])
        for i, w in enumerate((wqkv_q, wqkv_k, wqkv_v))
    ]
    for c in load_w:
        c.start()

    own_row = jnp.sum(moments_ref[...], axis=0, keepdims=True)
    mom[me] = jnp.broadcast_to(own_row, (8, 128))

    pl.semaphore_wait(barrier, has_left.astype(jnp.int32) + has_right.astype(jnp.int32))

    def mom_copy(s, right):
        return remote(
            mom.at[s],
            mom.at[s],
            mom_send.at[s, 1 if right else 0],
            mom_recv.at[s],
            me + 1 if right else me - 1,
        )

    @pl.when(has_right)
    def _():
        mom_copy(me, True).start()

    @pl.when(has_left)
    def _():
        mom_copy(me, False).start()

    def goes(right, p):
        if right:
            return has_right & jnp.logical_not(is_lent(n, p) & (me + 1 == last))
        return has_left & jnp.logical_not(is_lent(n, p) & (me - 1 == 0))

    def kv_copy(p, s, c, right, src=None):
        dst = kv.at[c, p, s]
        return remote(
            dst if src is None else src,
            dst,
            (send_r if right else send_l).at[p, s, c],
            recv.at[p, s, c],
            me + 1 if right else me - 1,
        )

    def send_own(p):
        cols = pl.ds(pl.multiple_of(p * PW, PW), PW)
        for right in (True, False):

            @pl.when(goes(right, p))
            def _():
                for c, ref in enumerate((keys_hbm, values_hbm)):
                    kv_copy(p, me, c, right, ref.at[:, cols]).start()

    for p in range(AHEAD):
        send_own(jnp.int32(p))

    load_conv = pltpu.make_async_copy(wconv_hbm, wconv, local_sem.at[4])
    load_conv.start()

    def own_copies(p):
        cols = pl.ds(pl.multiple_of(p * PW, PW), PW)
        return [
            pltpu.make_async_copy(ref.at[:, cols], kv.at[c, p, n], local_sem.at[5 + c])
            for c, ref in enumerate((keys_hbm, values_hbm))
        ]

    load_hid.wait()

    def column_sums(i, carry):
        a, b = carry
        x = hid[pl.ds(pl.multiple_of(i * W, W), W), :].astype(F32)
        return (
            a + jnp.sum(x, axis=0, keepdims=True),
            b + jnp.sum(x * x, axis=0, keepdims=True),
        )

    zero_row = jnp.zeros((1, chan), F32)
    sum_x, sum_xx = lax.fori_loop(0, tok // W, column_sums, (zero_row, zero_row))

    for j in range(1, n):

        @pl.when(me - j >= 0)
        def _():
            mom_copy(me - j, True).wait_recv()

            @pl.when(has_right)
            def _():
                mom_copy(me - j, True).start()

        @pl.when(me + j <= last)
        def _():
            mom_copy(me + j, False).wait_recv()

            @pl.when(has_left)
            def _():
                mom_copy(me + j, False).start()

    def others(s, row):
        return row + jnp.where(s == me, 0.0, mom[s])

    other_rows = lax.fori_loop(0, n, others, jnp.zeros((8, 128), F32))
    mom_total = jnp.broadcast_to(other_rows[0:1], (8, 128))

    group_of = lax.div(lax.broadcasted_iota(jnp.int32, (chan, 128), 0), chan // GROUPS)
    lane_of = lax.broadcasted_iota(jnp.int32, (chan, 128), 1)

    def spread(k):
        return (lane_of == group_of + k * GROUPS).astype(F32)

    def factors(norm, s_x, s_xx, gain, offset):
        e_sum, e_sq = spread(2 * norm), spread(2 * norm + 1)
        own = jnp.dot(
            jnp.broadcast_to(s_x, (8, chan)), e_sum, precision=HI, preferred_element_type=F32
        ) + jnp.dot(
            jnp.broadcast_to(s_xx, (8, chan)), e_sq, precision=HI, preferred_element_type=F32
        )
        totals = mom_total + own
        nt = (((1,), (1,)), ((), ()))
        first = lax.dot_general(totals, e_sum, nt, precision=HI, preferred_element_type=F32)
        second = lax.dot_general(totals, e_sq, nt, precision=HI, preferred_element_type=F32)
        average = first[0:1] / count
        variance = second[0:1] / count - average * average
        inverse = lax.rsqrt(variance + EPS)
        rows_n[0:1, :] = inverse * gain
        rows_n[1:2, :] = offset - average * inverse * gain

    factors(0, sum_x, sum_xx, gain_a[...], bias_a[...])

    def normalize(i, _):
        rows = pl.ds(pl.multiple_of(i * W, W), W)
        upd[rows, :] = (hid[rows, :].astype(F32) * rows_n[0:1, :] + rows_n[1:2, :]).astype(BF16)
        return 0

    lax.fori_loop(0, tok // W, normalize, 0)
    for c in load_w:
        c.wait()
    scale = (chan // HEADS) ** (-0.5)

    def project(j, _):
        cols = pl.ds(pl.multiple_of(j * 2 * PW, 2 * PW), 2 * PW)
        for i in range(3):
            r = jnp.dot(upd[...], wq[i, :, cols], preferred_element_type=F32).astype(BF16)
            for half in range(2):
                piece = r[:, half * PW : (half + 1) * PW]
                if i == 0:
                    q_ref[2 * j + half] = (piece.astype(F32) * scale).astype(BF16)
                else:
                    kv[i - 1, 2 * j + half, me] = piece
        return 0

    lax.fori_loop(0, chan // (2 * PW), project, 0)

    def q_copy(f):
        return remote(
            q_ref.at[2 * f + 2], q_in.at[f], lend_send.at[0, f], lend_recv.at[0, f], server
        )

    def lent_copy(f):
        return remote(
            lent_out.at[f], lent_in.at[f], lend_send.at[1, f], lend_recv.at[1, f], served
        )

    def stat_copy(f):
        return remote(
            stat_out.at[f], stat_in.at[f], lend_send.at[2, f], lend_recv.at[2, f], served
        )

    n_lent = q_in.shape[0]
    if n >= 4:

        @pl.when(is_end)
        def _():
            for f in range(n_lent):
                q_copy(f).start()

    lane = lax.broadcasted_iota(jnp.int32, (tok, PW), 1)

    def attend(q, p, shards, slot_of):
        q32 = q.astype(F32)
        halves = [
            jnp.where((lane >= h * 64) & (lane < h * 64 + 64), q32, 0.0).astype(BF16)
            for h in range(2)
        ]

        def score(j, tops):
            k = kv[0, p, slot_of(j)]
            new = []
            for h in range(2):
                sc = lax.dot_general(
                    k, halves[h], (((1,), (1,)), ((), ())), preferred_element_type=F32
                )
                sbuf[h, j] = sc
                new.append(jnp.maximum(tops[h], jnp.max(sc, axis=0, keepdims=True)))
            return tuple(new)

        low = jnp.full((1, tok), -jnp.inf, F32)
        tops = lax.fori_loop(0, shards, score, (low, low))

        def weigh(j, carry):
            v = kv[1, p, slot_of(j)]
            new = []
            for h in range(2):
                total, acc = carry[h]
                wts = jnp.exp(sbuf[h, j] - tops[h])
                part = lax.dot_general(
                    v[:, h * 64 : h * 64 + 64],
                    wts.astype(BF16),
                    (((0,), (0,)), ((), ())),
                    preferred_element_type=F32,
                )
                new.append((total + jnp.sum(wts, axis=0, keepdims=True), acc + part))
            return tuple(new)

        zero = (jnp.zeros((1, tok), F32), jnp.zeros((64, tok), F32))
        sums_h = lax.fori_loop(0, shards, weigh, (zero, zero))
        return [(tops[h], sums_h[h][0], sums_h[h][1]) for h in range(2)]

    def step(p, _):
        cols = pl.ds(pl.multiple_of(p * PW, PW), PW)
        lent = is_lent(n, p)
        f = lent_index(p)

        @pl.when(p + AHEAD < pairs)
        def _():
            send_own(p + AHEAD)

        serve = lent & is_server
        alone = lent & is_end

        @pl.when(serve)
        def _():
            for c in own_copies(p):
                c.start()

        @pl.when(jnp.logical_not(alone))
        def _():
            for j in range(1, n):

                @pl.when(me - j >= 0)
                def _():
                    for c in range(2):
                        kv_copy(p, me - j, c, True).wait_recv()

                        @pl.when(goes(True, p))
                        def _():
                            kv_copy(p, me - j, c, True).start()

                @pl.when(me + j <= last)
                def _():
                    for c in range(2):
                        kv_copy(p, me + j, c, False).wait_recv()

                        @pl.when(goes(False, p))
                        def _():
                            kv_copy(p, me + j, c, False).start()

        if n >= 4:

            @pl.when(serve)
            def _():
                for c in own_copies(p):
                    c.wait()
                q_copy(f).wait_recv()

                def slot(j):
                    s = j + jnp.where(served == 0, 1, 0)
                    return jnp.where(s == me, n, s)

                for h, (top, total, acc) in enumerate(attend(q_in[f], p, n - 1, slot)):
                    lent_out[f, h * 64 : h * 64 + 64, :] = (acc / total).astype(BF16)
                    stat_out[f, h : h + 1, :] = top
                    stat_out[f, 2 + h : 3 + h, :] = total
                stat_out[f, 4:8, :] = jnp.zeros((4, tok), F32)
                lent_copy(f).start()
                stat_copy(f).start()

        shards = jnp.where(alone, 1, n)
        mine = attend(q_ref[p], p, shards, lambda j: jnp.where(alone, me, j))

        @pl.when(jnp.logical_not(alone))
        def _():
            for h, (top, total, acc) in enumerate(mine):
                ot[h * 64 : h * 64 + 64, :] = acc / total

        if n >= 4:

            @pl.when(alone)
            def _():
                lent_copy(f).wait_recv()
                stat_copy(f).wait_recv()
                for h, (top, total, acc) in enumerate(mine):
                    top_b = stat_in[f, h : h + 1, :]
                    total_b = stat_in[f, 2 + h : 3 + h, :]
                    high = jnp.maximum(top, top_b)
                    fac_a = jnp.exp(top - high)
                    fac_b = jnp.exp(top_b - high) * total_b
                    got = lent_in[f, h * 64 : h * 64 + 64, :].astype(F32)
                    ot[h * 64 : h * 64 + 64, :] = (acc * fac_a + got * fac_b) / (
                        total * fac_a + fac_b
                    )

        new = (hid[:, cols].astype(F32) + ot[...].T).astype(BF16)
        upd[:, cols] = new
        new32 = new.astype(F32)
        sums[0:1, cols] = jnp.sum(new32, axis=0, keepdims=True)
        sums[1:2, cols] = jnp.sum(new32 * new32, axis=0, keepdims=True)
        return 0

    lax.fori_loop(0, pairs, step, 0)

    factors(1, sums[0:1, :], sums[1:2, :], gain_c[...], bias_c[...])
    image_rows = tok // W

    def activate(i):
        x = upd[pl.ds(pl.multiple_of(i * W, W), W), :].astype(F32)
        v = x * rows_n[0:1, :] + rows_n[1:2, :]
        act[pl.ds(pl.multiple_of(i * W + W, W), W), :] = (v / (1.0 + jnp.exp(-v))).astype(BF16)

    activate(jnp.int32(0))
    activate(jnp.int32(image_rows - 1))
    up = remote(
        act.at[pl.ds(W, W)],
        act.at[pl.ds(tok + W, W)],
        halo_send.at[0],
        halo_recv.at[0],
        me - 1,
    )
    down = remote(
        act.at[pl.ds(tok, W)], act.at[pl.ds(0, W)], halo_send.at[1], halo_recv.at[1], me + 1
    )

    @pl.when(has_left)
    def _():
        up.start()

    @pl.when(has_right)
    def _():
        down.start()

    lax.fori_loop(1, image_rows - 1, lambda i, c: (activate(i), c)[1], 0)
    load_conv.wait()

    def middle_tap(b, _):
        ybuf[b] = jnp.dot(act[W : W + tok, :], wconv[3 + b], preferred_element_type=F32)
        return 0

    lax.fori_loop(0, 3, middle_tap, 0)

    @pl.when(has_right)
    def _():
        up.wait_recv()

    @pl.when(jnp.logical_not(has_right))
    def _():
        act[tok + W : tok + 2 * W, :] = jnp.zeros((W, chan), BF16)

    @pl.when(has_left)
    def _():
        down.wait_recv()

    @pl.when(jnp.logical_not(has_left))
    def _():
        act[0:W, :] = jnp.zeros((W, chan), BF16)

    def outer_tap(t, _):
        a, b = lax.div(t, 3) * 2, lax.rem(t, 3)
        rows = pl.ds(pl.multiple_of(a * W, W), tok)
        ybuf[b] += jnp.dot(act[rows, :], wconv[a * 3 + b], preferred_element_type=F32)
        return 0

    lax.fori_loop(0, 6, outer_tap, 0)

    cout = out_ref.shape[1]
    column = lax.rem(lax.broadcasted_iota(jnp.int32, (tok, cout), 0), W)
    before = jnp.where(column == 0, 0.0, pltpu.roll(ybuf[0], 1, 0))
    after = jnp.where(column == W - 1, 0.0, pltpu.roll(ybuf[2], tok - 1, 0))
    out_ref[...] = (before + ybuf[1] + after + bias_out[...]).astype(BF16)

    def drain(p, _):
        for right in (True, False):
            for j in range(n):
                s = me - j if right else me + j
                ok = (s >= 0) if right else (s <= last)

                @pl.when(goes(right, p) & ok)
                def _():
                    for c in range(2):
                        kv_copy(p, s, c, right).wait_send()

        return 0

    lax.fori_loop(0, pairs, drain, 0)
    for j in range(n):

        @pl.when(has_right & (me - j >= 0))
        def _():
            mom_copy(me - j, True).wait_send()

        @pl.when(has_left & (me + j <= last))
        def _():
            mom_copy(me + j, False).wait_send()

    if n >= 4:

        @pl.when(is_end)
        def _():
            for f in range(n_lent):
                q_copy(f).wait_send()

        @pl.when(is_server)
        def _():
            for f in range(n_lent):
                lent_copy(f).wait_send()
                stat_copy(f).wait_send()

    @pl.when(has_left)
    def _():
        up.wait_send()

    @pl.when(has_right)
    def _():
        down.wait_send()


def time_embedding(timestep, w_time):
    half_dim = w_time.shape[0] // 2
    frequency = jnp.exp(-math.log(10000.0) * jnp.arange(half_dim, dtype=jnp.float32) / half_dim)
    angles = timestep[0].astype(jnp.float32) * frequency
    embedded = jnp.concatenate([jnp.cos(angles), jnp.sin(angles)])
    return jnp.dot(embedded[None, :], w_time.astype(jnp.float32), precision=lax.Precision.HIGHEST)


def body(
    n,
    hidden_in,
    stale_keys,
    stale_values,
    stale_moments,
    gain_attn,
    bias_attn,
    w_query,
    w_key,
    w_value,
    gain_conv,
    bias_conv,
    conv_weight,
    conv_bias,
    w_time,
    timestep,
):
    tok, chan = hidden_in.shape
    cout = conv_weight.shape[3]
    pairs = chan // PW
    lent = 4
    bias_out = time_embedding(timestep, w_time) + conv_bias[None, :]
    vmem = pl.BlockSpec(memory_space=pltpu.VMEM)
    hbm = pl.BlockSpec(memory_space=pl.ANY)
    dma = pltpu.SemaphoreType.DMA
    return pl.pallas_call(
        functools.partial(kernel, n),
        out_shape=jax.ShapeDtypeStruct((tok, cout), BF16),
        in_specs=[hbm] * 3 + [vmem] * 5 + [hbm] * 4 + [vmem],
        out_specs=vmem,
        scratch_shapes=[
            pltpu.VMEM((tok, chan), BF16),
            pltpu.VMEM((3, chan, chan), BF16),
            pltpu.VMEM((9, chan, cout), BF16),
            pltpu.VMEM((2, pairs, n + 1, tok, PW), BF16),
            pltpu.VMEM((pairs, tok, PW), BF16),
            pltpu.VMEM((lent, tok, PW), BF16),
            pltpu.VMEM((lent, PW, tok), BF16),
            pltpu.VMEM((lent, PW, tok), BF16),
            pltpu.VMEM((lent, 8, tok), F32),
            pltpu.VMEM((lent, 8, tok), F32),
            pltpu.VMEM((2, n, tok, tok), F32),
            pltpu.VMEM((PW, tok), F32),
            pltpu.VMEM((tok, chan), BF16),
            pltpu.VMEM((tok + 2 * W, chan), BF16),
            pltpu.VMEM((3, tok, cout), F32),
            pltpu.VMEM((8, chan), F32),
            pltpu.VMEM((8, chan), F32),
            pltpu.VMEM((n, 8, 128), F32),
            dma((8,)),
            dma((pairs, n, 2)),
            dma((pairs, n, 2)),
            dma((pairs, n, 2)),
            dma((n, 2)),
            dma((n,)),
            dma((3, lent)),
            dma((3, lent)),
            dma((2,)),
            dma((2,)),
        ],
        compiler_params=pltpu.CompilerParams(
            collective_id=0,
            has_side_effects=True,
            vmem_limit_bytes=63 * 1024 * 1024,
        ),
        cost_estimate=pl.CostEstimate(
            flops=2 * tok * chan * (3 * chan + 2 * n * tok + 9 * cout),
            bytes_accessed=2 * (3 * chan * chan + 9 * chan * cout + 4 * tok * chan),
            transcendentals=HEADS * n * tok * tok,
        ),
    )(
        hidden_in,
        stale_keys,
        stale_values,
        stale_moments.reshape(stale_moments.shape[0], 128),
        gain_attn[None, :],
        bias_attn[None, :],
        gain_conv[None, :],
        bias_conv[None, :],
        w_query,
        w_key,
        w_value,
        conv_weight.reshape(9, chan, cout),
        bias_out,
    )


def solution(mesh):
    split = P(("batch", "patch"), None)
    return jax.shard_map(
        functools.partial(body, mesh.shape["patch"]),
        mesh=mesh,
        in_specs=(split, split, split, P(("batch", "patch"), None, None, None)) + (P(),) * 11,
        out_specs=split,
        check_vma=False,
    )
```

```python
import functools
import math

import jax
import jax.numpy as jnp
from jax import lax
from jax.experimental import pallas as pl
from jax.experimental.pallas import tpu as pltpu
from jax.sharding import PartitionSpec as P

HEADS = 20
GROUPS = 32
W = 64
EPS = 1e-05
PW = 128
F32 = jnp.float32
BF16 = jnp.bfloat16
HI = lax.Precision.HIGHEST


def is_lent(n, p):
    if n < 4:
        return p < 0
    return (lax.rem(p, 2) == 0) & (p >= 2)


def lent_index(p):
    return jnp.maximum(lax.div(p, 2) - 1, 0)


def kernel(
    n,
    hidden_hbm,
    keys_hbm,
    values_hbm,
    moments_ref,
    gain_a,
    bias_a,
    gain_c,
    bias_c,
    wqkv_q,
    wqkv_k,
    wqkv_v,
    wconv_hbm,
    bias_out,
    out_ref,
    hid,
    wq,
    wconv,
    kv,
    q_ref,
    q_in,
    lent_out,
    lent_in,
    stat_out,
    stat_in,
    sbuf,
    ot,
    upd,
    act,
    ybuf,
    sums,
    rows_n,
    mom,
    local_sem,
    send_r,
    send_l,
    recv,
    mom_send,
    mom_recv,
    lend_send,
    lend_recv,
    halo_send,
    halo_recv,
):
    me = lax.axis_index("patch")
    tok, chan = hid.shape
    pairs = chan // PW
    count = n * tok * (chan // GROUPS)
    last = n - 1
    has_left, has_right = me > 0, me < last
    is_end = (me == 0) | (me == last)
    is_server = ((me == 1) | (me == n - 2)) if n >= 4 else (me < 0)
    served = jnp.where(me == 1, 0, last)
    server = jnp.where(me == 0, 1, last - 1)

    def remote(src, dst, ssem, rsem, to):
        return pltpu.make_async_remote_copy(
            src_ref=src,
            dst_ref=dst,
            send_sem=ssem,
            recv_sem=rsem,
            device_id={"patch": to},
            device_id_type=pl.DeviceIdType.MESH,
        )

    barrier = pltpu.get_barrier_semaphore()

    @pl.when(has_left)
    def _():
        pl.semaphore_signal(
            barrier, inc=1, device_id={"patch": me - 1}, device_id_type=pl.DeviceIdType.MESH
        )

    @pl.when(has_right)
    def _():
        pl.semaphore_signal(
            barrier, inc=1, device_id={"patch": me + 1}, device_id_type=pl.DeviceIdType.MESH
        )

    load_hid = pltpu.make_async_copy(hidden_hbm, hid, local_sem.at[0])
    load_hid.start()
    load_w = [
        pltpu.make_async_copy(w, wq.at[i], local_sem.at[1 + i])
        for i, w in enumerate((wqkv_q, wqkv_k, wqkv_v))
    ]
    for c in load_w:
        c.start()

    own_row = jnp.sum(moments_ref[...], axis=0, keepdims=True)
    mom[me] = jnp.broadcast_to(own_row, (8, 128))

    pl.semaphore_wait(barrier, has_left.astype(jnp.int32) + has_right.astype(jnp.int32))

    def mom_copy(s, right):
        return remote(
            mom.at[s],
            mom.at[s],
            mom_send.at[s, 1 if right else 0],
            mom_recv.at[s],
            me + 1 if right else me - 1,
        )

    @pl.when(has_right)
    def _():
        mom_copy(me, True).start()

    @pl.when(has_left)
    def _():
        mom_copy(me, False).start()

    def goes(right, p):
        if right:
            return has_right & jnp.logical_not(is_lent(n, p) & (me + 1 == last))
        return has_left & jnp.logical_not(is_lent(n, p) & (me - 1 == 0))

    def kv_copy(p, s, c, right, src=None):
        dst = kv.at[c, p, s]
        return remote(
            dst if src is None else src,
            dst,
            (send_r if right else send_l).at[p, s, c],
            recv.at[p, s, c],
            me + 1 if right else me - 1,
        )

    def send_own(p):
        cols = pl.ds(pl.multiple_of(p * PW, PW), PW)
        for right in (True, False):

            @pl.when(goes(right, p))
            def _():
                for c, ref in enumerate((keys_hbm, values_hbm)):
                    kv_copy(p, me, c, right, ref.at[:, cols]).start()

    def forward(p, j):
        @pl.when(has_right & (me - j >= 0))
        def _():
            for c in range(2):
                kv_copy(p, me - j, c, True).wait_recv()

                @pl.when(goes(True, p))
                def _():
                    kv_copy(p, me - j, c, True).start()

        @pl.when(has_left & (me + j <= last))
        def _():
            for c in range(2):
                kv_copy(p, me + j, c, False).wait_recv()

                @pl.when(goes(False, p))
                def _():
                    kv_copy(p, me + j, c, False).start()

    def pump(t):
        @pl.when(t < pairs)
        def _():
            send_own(t)

        for j in range(1, n - 1):

            @pl.when((t - j >= 0) & (t - j < pairs))
            def _():
                forward(t - j, j)

    send_own(jnp.int32(0))
    send_own(jnp.int32(1))

    load_conv = pltpu.make_async_copy(wconv_hbm, wconv, local_sem.at[4])
    load_conv.start()

    def own_copies(p):
        cols = pl.ds(pl.multiple_of(p * PW, PW), PW)
        return [
            pltpu.make_async_copy(ref.at[:, cols], kv.at[c, p, n], local_sem.at[5 + c])
            for c, ref in enumerate((keys_hbm, values_hbm))
        ]

    load_hid.wait()

    def column_sums(i, carry):
        a, b = carry
        x = hid[pl.ds(pl.multiple_of(i * W, W), W), :].astype(F32)
        return (
            a + jnp.sum(x, axis=0, keepdims=True),
            b + jnp.sum(x * x, axis=0, keepdims=True),
        )

    zero_row = jnp.zeros((1, chan), F32)
    sum_x, sum_xx = lax.fori_loop(0, tok // W, column_sums, (zero_row, zero_row))

    for j in range(1, n):

        @pl.when(me - j >= 0)
        def _():
            mom_copy(me - j, True).wait_recv()

            @pl.when(has_right)
            def _():
                mom_copy(me - j, True).start()

        @pl.when(me + j <= last)
        def _():
            mom_copy(me + j, False).wait_recv()

            @pl.when(has_left)
            def _():
                mom_copy(me + j, False).start()

    def others(s, row):
        return row + jnp.where(s == me, 0.0, mom[s])

    other_rows = lax.fori_loop(0, n, others, jnp.zeros((8, 128), F32))
    mom_total = jnp.broadcast_to(other_rows[0:1], (8, 128))

    group_of = lax.div(lax.broadcasted_iota(jnp.int32, (chan, 128), 0), chan // GROUPS)
    lane_of = lax.broadcasted_iota(jnp.int32, (chan, 128), 1)

    def spread(k):
        return (lane_of == group_of + k * GROUPS).astype(F32)

    def factors(norm, s_x, s_xx, gain, offset):
        e_sum, e_sq = spread(2 * norm), spread(2 * norm + 1)
        own = jnp.dot(
            jnp.broadcast_to(s_x, (8, chan)), e_sum, precision=HI, preferred_element_type=F32
        ) + jnp.dot(
            jnp.broadcast_to(s_xx, (8, chan)), e_sq, precision=HI, preferred_element_type=F32
        )
        totals = mom_total + own
        nt = (((1,), (1,)), ((), ()))
        first = lax.dot_general(totals, e_sum, nt, precision=HI, preferred_element_type=F32)
        second = lax.dot_general(totals, e_sq, nt, precision=HI, preferred_element_type=F32)
        average = first[0:1] / count
        variance = second[0:1] / count - average * average
        inverse = lax.rsqrt(variance + EPS)
        rows_n[0:1, :] = inverse * gain
        rows_n[1:2, :] = offset - average * inverse * gain

    factors(0, sum_x, sum_xx, gain_a[...], bias_a[...])

    def normalize(i, _):
        rows = pl.ds(pl.multiple_of(i * W, W), W)
        upd[rows, :] = (hid[rows, :].astype(F32) * rows_n[0:1, :] + rows_n[1:2, :]).astype(BF16)
        return 0

    lax.fori_loop(0, tok // W, normalize, 0)
    for c in load_w:
        c.wait()
    for j in range(1, n - 1):
        if j < 2:
            forward(jnp.int32(0), j)
    scale = (chan // HEADS) ** (-0.5)

    def project(j, _):
        @pl.when(j == 2)
        def _():
            for t in range(2, n - 1):
                pump(jnp.int32(t))

        cols = pl.ds(pl.multiple_of(j * 2 * PW, 2 * PW), 2 * PW)
        for i in range(3):
            r = jnp.dot(upd[...], wq[i, :, cols], preferred_element_type=F32).astype(BF16)
            for half in range(2):
                piece = r[:, half * PW : (half + 1) * PW]
                if i == 0:
                    q_ref[2 * j + half] = (piece.astype(F32) * scale).astype(BF16)
                else:
                    kv[i - 1, 2 * j + half, me] = piece
        return 0

    lax.fori_loop(0, chan // (2 * PW), project, 0)

    def q_copy(f):
        return remote(
            q_ref.at[2 * f + 2], q_in.at[f], lend_send.at[0, f], lend_recv.at[0, f], server
        )

    def lent_copy(f):
        return remote(
            lent_out.at[f], lent_in.at[f], lend_send.at[1, f], lend_recv.at[1, f], served
        )

    def stat_copy(f):
        return remote(
            stat_out.at[f], stat_in.at[f], lend_send.at[2, f], lend_recv.at[2, f], served
        )

    n_lent = q_in.shape[0]
    if n >= 4:

        @pl.when(is_end)
        def _():
            for f in range(n_lent):
                q_copy(f).start()

    lane = lax.broadcasted_iota(jnp.int32, (tok, PW), 1)

    def attend(q, p, shards, slot_of):
        q32 = q.astype(F32)
        halves = [
            jnp.where((lane >= h * 64) & (lane < h * 64 + 64), q32, 0.0).astype(BF16)
            for h in range(2)
        ]

        def score(j, tops):
            k = kv[0, p, slot_of(j)]
            new = []
            for h in range(2):
                sc = lax.dot_general(
                    k, halves[h], (((1,), (1,)), ((), ())), preferred_element_type=F32
                )
                sbuf[h, j] = sc
                new.append(jnp.maximum(tops[h], jnp.max(sc, axis=0, keepdims=True)))
            return tuple(new)

        low = jnp.full((1, tok), -jnp.inf, F32)
        tops = lax.fori_loop(0, shards, score, (low, low))

        def weigh(j, carry):
            v = kv[1, p, slot_of(j)]
            new = []
            for h in range(2):
                total, acc = carry[h]
                wts = jnp.exp(sbuf[h, j] - tops[h])
                part = lax.dot_general(
                    v[:, h * 64 : h * 64 + 64],
                    wts.astype(BF16),
                    (((0,), (0,)), ((), ())),
                    preferred_element_type=F32,
                )
                new.append((total + jnp.sum(wts, axis=0, keepdims=True), acc + part))
            return tuple(new)

        zero = (jnp.zeros((1, tok), F32), jnp.zeros((64, tok), F32))
        sums_h = lax.fori_loop(0, shards, weigh, (zero, zero))
        return [(tops[h], sums_h[h][0], sums_h[h][1]) for h in range(2)]

    def step(p, _):
        cols = pl.ds(pl.multiple_of(p * PW, PW), PW)
        lent = is_lent(n, p)
        f = lent_index(p)

        pump(p + n - 1)

        serve = lent & is_server
        alone = lent & is_end

        @pl.when(serve)
        def _():
            for c in own_copies(p):
                c.start()

        for j in range(1, n):

            @pl.when(jnp.logical_not(alone | has_right) & (me - j >= 0))
            def _():
                for c in range(2):
                    kv_copy(p, me - j, c, True).wait_recv()

            @pl.when(jnp.logical_not(alone | has_left) & (me + j <= last))
            def _():
                for c in range(2):
                    kv_copy(p, me + j, c, False).wait_recv()

        if n >= 4:

            @pl.when(serve)
            def _():
                for c in own_copies(p):
                    c.wait()
                q_copy(f).wait_recv()

                def slot(j):
                    s = j + jnp.where(served == 0, 1, 0)
                    return jnp.where(s == me, n, s)

                for h, (top, total, acc) in enumerate(attend(q_in[f], p, n - 1, slot)):
                    lent_out[f, h * 64 : h * 64 + 64, :] = (acc / total).astype(BF16)
                    stat_out[f, h : h + 1, :] = top
                    stat_out[f, 2 + h : 3 + h, :] = total
                stat_out[f, 4:8, :] = jnp.zeros((4, tok), F32)
                lent_copy(f).start()
                stat_copy(f).start()

        shards = jnp.where(alone, 1, n)
        mine = attend(q_ref[p], p, shards, lambda j: jnp.where(alone, me, j))

        @pl.when(jnp.logical_not(alone))
        def _():
            for h, (top, total, acc) in enumerate(mine):
                ot[h * 64 : h * 64 + 64, :] = acc / total

        if n >= 4:

            @pl.when(alone)
            def _():
                lent_copy(f).wait_recv()
                stat_copy(f).wait_recv()
                for h, (top, total, acc) in enumerate(mine):
                    top_b = stat_in[f, h : h + 1, :]
                    total_b = stat_in[f, 2 + h : 3 + h, :]
                    high = jnp.maximum(top, top_b)
                    fac_a = jnp.exp(top - high)
                    fac_b = jnp.exp(top_b - high) * total_b
                    got = lent_in[f, h * 64 : h * 64 + 64, :].astype(F32)
                    ot[h * 64 : h * 64 + 64, :] = (acc * fac_a + got * fac_b) / (
                        total * fac_a + fac_b
                    )

        new = (hid[:, cols].astype(F32) + ot[...].T).astype(BF16)
        upd[:, cols] = new
        new32 = new.astype(F32)
        sums[0:1, cols] = jnp.sum(new32, axis=0, keepdims=True)
        sums[1:2, cols] = jnp.sum(new32 * new32, axis=0, keepdims=True)
        return 0

    lax.fori_loop(0, pairs, step, 0)

    factors(1, sums[0:1, :], sums[1:2, :], gain_c[...], bias_c[...])
    image_rows = tok // W

    def activate(i):
        x = upd[pl.ds(pl.multiple_of(i * W, W), W), :].astype(F32)
        v = x * rows_n[0:1, :] + rows_n[1:2, :]
        act[pl.ds(pl.multiple_of(i * W + W, W), W), :] = (v / (1.0 + jnp.exp(-v))).astype(BF16)

    activate(jnp.int32(0))
    activate(jnp.int32(image_rows - 1))
    up = remote(
        act.at[pl.ds(W, W)],
        act.at[pl.ds(tok + W, W)],
        halo_send.at[0],
        halo_recv.at[0],
        me - 1,
    )
    down = remote(
        act.at[pl.ds(tok, W)], act.at[pl.ds(0, W)], halo_send.at[1], halo_recv.at[1], me + 1
    )

    @pl.when(has_left)
    def _():
        up.start()

    @pl.when(has_right)
    def _():
        down.start()

    lax.fori_loop(1, image_rows - 1, lambda i, c: (activate(i), c)[1], 0)
    load_conv.wait()

    def middle_tap(b, _):
        ybuf[b] = jnp.dot(act[W : W + tok, :], wconv[3 + b], preferred_element_type=F32)
        return 0

    lax.fori_loop(0, 3, middle_tap, 0)

    @pl.when(has_right)
    def _():
        up.wait_recv()

    @pl.when(jnp.logical_not(has_right))
    def _():
        act[tok + W : tok + 2 * W, :] = jnp.zeros((W, chan), BF16)

    @pl.when(has_left)
    def _():
        down.wait_recv()

    @pl.when(jnp.logical_not(has_left))
    def _():
        act[0:W, :] = jnp.zeros((W, chan), BF16)

    def outer_tap(t, _):
        a, b = lax.div(t, 3) * 2, lax.rem(t, 3)
        rows = pl.ds(pl.multiple_of(a * W, W), tok)
        ybuf[b] += jnp.dot(act[rows, :], wconv[a * 3 + b], preferred_element_type=F32)
        return 0

    lax.fori_loop(0, 6, outer_tap, 0)

    cout = out_ref.shape[1]
    column = lax.rem(lax.broadcasted_iota(jnp.int32, (tok, cout), 0), W)
    before = jnp.where(column == 0, 0.0, pltpu.roll(ybuf[0], 1, 0))
    after = jnp.where(column == W - 1, 0.0, pltpu.roll(ybuf[2], tok - 1, 0))
    out_ref[...] = (before + ybuf[1] + after + bias_out[...]).astype(BF16)

    def drain(p, _):
        for right in (True, False):
            for j in range(n):
                s = me - j if right else me + j
                ok = (s >= 0) if right else (s <= last)

                @pl.when(goes(right, p) & ok)
                def _():
                    for c in range(2):
                        kv_copy(p, s, c, right).wait_send()

        return 0

    lax.fori_loop(0, pairs, drain, 0)
    for j in range(n):

        @pl.when(has_right & (me - j >= 0))
        def _():
            mom_copy(me - j, True).wait_send()

        @pl.when(has_left & (me + j <= last))
        def _():
            mom_copy(me + j, False).wait_send()

    if n >= 4:

        @pl.when(is_end)
        def _():
            for f in range(n_lent):
                q_copy(f).wait_send()

        @pl.when(is_server)
        def _():
            for f in range(n_lent):
                lent_copy(f).wait_send()
                stat_copy(f).wait_send()

    @pl.when(has_left)
    def _():
        up.wait_send()

    @pl.when(has_right)
    def _():
        down.wait_send()


def time_embedding(timestep, w_time):
    half_dim = w_time.shape[0] // 2
    frequency = jnp.exp(-math.log(10000.0) * jnp.arange(half_dim, dtype=jnp.float32) / half_dim)
    angles = timestep[0].astype(jnp.float32) * frequency
    embedded = jnp.concatenate([jnp.cos(angles), jnp.sin(angles)])
    return jnp.dot(embedded[None, :], w_time.astype(jnp.float32), precision=lax.Precision.HIGHEST)


def body(
    n,
    hidden_in,
    stale_keys,
    stale_values,
    stale_moments,
    gain_attn,
    bias_attn,
    w_query,
    w_key,
    w_value,
    gain_conv,
    bias_conv,
    conv_weight,
    conv_bias,
    w_time,
    timestep,
):
    tok, chan = hidden_in.shape
    cout = conv_weight.shape[3]
    pairs = chan // PW
    lent = 4
    bias_out = time_embedding(timestep, w_time) + conv_bias[None, :]
    vmem = pl.BlockSpec(memory_space=pltpu.VMEM)
    hbm = pl.BlockSpec(memory_space=pl.ANY)
    dma = pltpu.SemaphoreType.DMA
    return pl.pallas_call(
        functools.partial(kernel, n),
        out_shape=jax.ShapeDtypeStruct((tok, cout), BF16),
        in_specs=[hbm] * 3 + [vmem] * 5 + [hbm] * 4 + [vmem],
        out_specs=vmem,
        scratch_shapes=[
            pltpu.VMEM((tok, chan), BF16),
            pltpu.VMEM((3, chan, chan), BF16),
            pltpu.VMEM((9, chan, cout), BF16),
            pltpu.VMEM((2, pairs, n + 1, tok, PW), BF16),
            pltpu.VMEM((pairs, tok, PW), BF16),
            pltpu.VMEM((lent, tok, PW), BF16),
            pltpu.VMEM((lent, PW, tok), BF16),
            pltpu.VMEM((lent, PW, tok), BF16),
            pltpu.VMEM((lent, 8, tok), F32),
            pltpu.VMEM((lent, 8, tok), F32),
            pltpu.VMEM((2, n, tok, tok), F32),
            pltpu.VMEM((PW, tok), F32),
            pltpu.VMEM((tok, chan), BF16),
            pltpu.VMEM((tok + 2 * W, chan), BF16),
            pltpu.VMEM((3, tok, cout), F32),
            pltpu.VMEM((8, chan), F32),
            pltpu.VMEM((8, chan), F32),
            pltpu.VMEM((n, 8, 128), F32),
            dma((8,)),
            dma((pairs, n, 2)),
            dma((pairs, n, 2)),
            dma((pairs, n, 2)),
            dma((n, 2)),
            dma((n,)),
            dma((3, lent)),
            dma((3, lent)),
            dma((2,)),
            dma((2,)),
        ],
        compiler_params=pltpu.CompilerParams(
            collective_id=0,
            has_side_effects=True,
            vmem_limit_bytes=63 * 1024 * 1024,
        ),
        cost_estimate=pl.CostEstimate(
            flops=2 * tok * chan * (3 * chan + 2 * n * tok + 9 * cout),
            bytes_accessed=2 * (3 * chan * chan + 9 * chan * cout + 4 * tok * chan),
            transcendentals=HEADS * n * tok * tok,
        ),
    )(
        hidden_in,
        stale_keys,
        stale_values,
        stale_moments.reshape(stale_moments.shape[0], 128),
        gain_attn[None, :],
        bias_attn[None, :],
        gain_conv[None, :],
        bias_conv[None, :],
        w_query,
        w_key,
        w_value,
        conv_weight.reshape(9, chan, cout),
        bias_out,
    )


def solution(mesh):
    split = P(("batch", "patch"), None)
    return jax.shard_map(
        functools.partial(body, mesh.shape["patch"]),
        mesh=mesh,
        in_specs=(split, split, split, P(("batch", "patch"), None, None, None)) + (P(),) * 11,
        out_specs=split,
        check_vma=False,
    )
```

```python
import functools
import math

import jax
import jax.numpy as jnp
from jax import lax
from jax.experimental import pallas as pl
from jax.experimental.pallas import tpu as pltpu
from jax.sharding import PartitionSpec as P

HEADS = 20
GROUPS = 32
W = 64
EPS = 1e-05
PW = 128
F32 = jnp.float32
BF16 = jnp.bfloat16
HI = lax.Precision.HIGHEST


def is_lent(n, p):
    if n < 4:
        return p < 0
    return (lax.rem(p, 2) == 0) & (p >= 2)


def lent_index(p):
    return jnp.maximum(lax.div(p, 2) - 1, 0)


def kernel(
    n,
    hidden_hbm,
    keys_hbm,
    values_hbm,
    moments_hbm,
    params,
    wqkv_q,
    wqkv_k,
    wqkv_v,
    wconv_hbm,
    out_ref,
    hid,
    wq,
    wconv,
    kv,
    q_ref,
    q_in,
    lent_out,
    lent_in,
    stat_out,
    stat_in,
    sbuf,
    ot,
    upd,
    act,
    ybuf,
    sums,
    rows_n,
    mom,
    mom_own,
    local_sem,
    send_r,
    send_l,
    recv,
    mom_send,
    mom_recv,
    lend_send,
    lend_recv,
    halo_send,
    halo_recv,
):
    me = lax.axis_index("patch")
    tok, chan = hid.shape
    pairs = chan // PW
    count = n * tok * (chan // GROUPS)
    last = n - 1
    has_left, has_right = me > 0, me < last
    is_end = (me == 0) | (me == last)
    is_server = ((me == 1) | (me == n - 2)) if n >= 4 else (me < 0)
    served = jnp.where(me == 1, 0, last)
    server = jnp.where(me == 0, 1, last - 1)

    def remote(src, dst, ssem, rsem, to):
        return pltpu.make_async_remote_copy(
            src_ref=src,
            dst_ref=dst,
            send_sem=ssem,
            recv_sem=rsem,
            device_id={"patch": to},
            device_id_type=pl.DeviceIdType.MESH,
        )

    barrier = pltpu.get_barrier_semaphore()

    @pl.when(has_left)
    def _():
        pl.semaphore_signal(
            barrier, inc=1, device_id={"patch": me - 1}, device_id_type=pl.DeviceIdType.MESH
        )

    @pl.when(has_right)
    def _():
        pl.semaphore_signal(
            barrier, inc=1, device_id={"patch": me + 1}, device_id_type=pl.DeviceIdType.MESH
        )

    load_hid = pltpu.make_async_copy(hidden_hbm, hid, local_sem.at[0])
    load_hid.start()
    load_mom = pltpu.make_async_copy(moments_hbm, mom_own, local_sem.at[7])
    load_mom.start()
    load_w = [
        pltpu.make_async_copy(w, wq.at[i], local_sem.at[1 + i])
        for i, w in enumerate((wqkv_q, wqkv_k, wqkv_v))
    ]
    for c in load_w:
        c.start()

    load_mom.wait()
    own4 = jnp.sum(mom_own[...], axis=0)
    own_row = jnp.concatenate(
        [own4[i, k : k + 1, :] for i in range(2) for k in range(2)], axis=1
    )
    mom[me] = jnp.broadcast_to(own_row, (8, 128))

    pl.semaphore_wait(barrier, has_left.astype(jnp.int32) + has_right.astype(jnp.int32))

    def mom_copy(s, right):
        return remote(
            mom.at[s],
            mom.at[s],
            mom_send.at[s, 1 if right else 0],
            mom_recv.at[s],
            me + 1 if right else me - 1,
        )

    @pl.when(has_right)
    def _():
        mom_copy(me, True).start()

    @pl.when(has_left)
    def _():
        mom_copy(me, False).start()

    def goes(right, p):
        if right:
            return has_right & jnp.logical_not(is_lent(n, p) & (me + 1 == last))
        return has_left & jnp.logical_not(is_lent(n, p) & (me - 1 == 0))

    def kv_copy(p, s, c, right, src=None):
        dst = kv.at[c, p, s]
        return remote(
            dst if src is None else src,
            dst,
            (send_r if right else send_l).at[p, s, c],
            recv.at[p, s, c],
            me + 1 if right else me - 1,
        )

    def send_own(p):
        cols = pl.ds(pl.multiple_of(p * PW, PW), PW)
        for right in (True, False):

            @pl.when(goes(right, p))
            def _():
                for c, ref in enumerate((keys_hbm, values_hbm)):
                    kv_copy(p, me, c, right, ref.at[:, cols]).start()

    def forward(p, j):
        @pl.when(has_right & (me - j >= 0))
        def _():
            for c in range(2):
                kv_copy(p, me - j, c, True).wait_recv()

                @pl.when(goes(True, p))
                def _():
                    kv_copy(p, me - j, c, True).start()

        @pl.when(has_left & (me + j <= last))
        def _():
            for c in range(2):
                kv_copy(p, me + j, c, False).wait_recv()

                @pl.when(goes(False, p))
                def _():
                    kv_copy(p, me + j, c, False).start()

    def pump(t):
        @pl.when(t < pairs)
        def _():
            send_own(t)

        for j in range(1, n - 1):

            @pl.when((t - j >= 0) & (t - j < pairs))
            def _():
                forward(t - j, j)

    send_own(jnp.int32(0))
    send_own(jnp.int32(1))

    load_conv = pltpu.make_async_copy(wconv_hbm, wconv, local_sem.at[4])
    load_conv.start()

    def own_copies(p):
        cols = pl.ds(pl.multiple_of(p * PW, PW), PW)
        return [
            pltpu.make_async_copy(ref.at[:, cols], kv.at[c, p, n], local_sem.at[5 + c])
            for c, ref in enumerate((keys_hbm, values_hbm))
        ]

    load_hid.wait()

    def column_sums(i, carry):
        a, b = carry
        x = hid[pl.ds(pl.multiple_of(i * W, W), W), :].astype(F32)
        return (
            a + jnp.sum(x, axis=0, keepdims=True),
            b + jnp.sum(x * x, axis=0, keepdims=True),
        )

    zero_row = jnp.zeros((1, chan), F32)
    sum_x, sum_xx = lax.fori_loop(0, tok // W, column_sums, (zero_row, zero_row))

    for j in range(1, n):

        @pl.when(me - j >= 0)
        def _():
            mom_copy(me - j, True).wait_recv()

            @pl.when(has_right)
            def _():
                mom_copy(me - j, True).start()

        @pl.when(me + j <= last)
        def _():
            mom_copy(me + j, False).wait_recv()

            @pl.when(has_left)
            def _():
                mom_copy(me + j, False).start()

    def others(s, row):
        return row + jnp.where(s == me, 0.0, mom[s])

    other_rows = lax.fori_loop(0, n, others, jnp.zeros((8, 128), F32))
    mom_total = jnp.broadcast_to(other_rows[0:1], (8, 128))

    group_of = lax.div(lax.broadcasted_iota(jnp.int32, (chan, 128), 0), chan // GROUPS)
    lane_of = lax.broadcasted_iota(jnp.int32, (chan, 128), 1)

    def spread(k):
        return (lane_of == group_of + k * GROUPS).astype(F32)

    def factors(norm, s_x, s_xx, gain, offset):
        e_sum, e_sq = spread(2 * norm), spread(2 * norm + 1)
        own = jnp.dot(
            jnp.broadcast_to(s_x, (8, chan)), e_sum, precision=HI, preferred_element_type=F32
        ) + jnp.dot(
            jnp.broadcast_to(s_xx, (8, chan)), e_sq, precision=HI, preferred_element_type=F32
        )
        totals = mom_total + own
        nt = (((1,), (1,)), ((), ()))
        first = lax.dot_general(totals, e_sum, nt, precision=HI, preferred_element_type=F32)
        second = lax.dot_general(totals, e_sq, nt, precision=HI, preferred_element_type=F32)
        average = first[0:1] / count
        variance = second[0:1] / count - average * average
        inverse = lax.rsqrt(variance + EPS)
        rows_n[0:1, :] = inverse * gain
        rows_n[1:2, :] = offset - average * inverse * gain

    factors(0, sum_x, sum_xx, params[0:1, :], params[1:2, :])

    def normalize(i, _):
        rows = pl.ds(pl.multiple_of(i * W, W), W)
        upd[rows, :] = (hid[rows, :].astype(F32) * rows_n[0:1, :] + rows_n[1:2, :]).astype(BF16)
        return 0

    lax.fori_loop(0, tok // W, normalize, 0)
    for c in load_w:
        c.wait()
    for j in range(1, n - 1):
        if j < 2:
            forward(jnp.int32(0), j)
    scale = (chan // HEADS) ** (-0.5)

    def project(j, _):
        @pl.when(j == 2)
        def _():
            for t in range(2, n - 1):
                pump(jnp.int32(t))

        cols = pl.ds(pl.multiple_of(j * 2 * PW, 2 * PW), 2 * PW)
        for i in range(3):
            r = jnp.dot(upd[...], wq[i, :, cols], preferred_element_type=F32).astype(BF16)
            for half in range(2):
                piece = r[:, half * PW : (half + 1) * PW]
                if i == 0:
                    q_ref[2 * j + half] = (piece.astype(F32) * scale).astype(BF16)
                else:
                    kv[i - 1, 2 * j + half, me] = piece
        return 0

    lax.fori_loop(0, chan // (2 * PW), project, 0)

    def q_copy(f):
        return remote(
            q_ref.at[2 * f + 2], q_in.at[f], lend_send.at[0, f], lend_recv.at[0, f], server
        )

    def lent_copy(f):
        return remote(
            lent_out.at[f], lent_in.at[f], lend_send.at[1, f], lend_recv.at[1, f], served
        )

    def stat_copy(f):
        return remote(
            stat_out.at[f], stat_in.at[f], lend_send.at[2, f], lend_recv.at[2, f], served
        )

    n_lent = q_in.shape[0]
    if n >= 4:

        @pl.when(is_end)
        def _():
            for f in range(n_lent):
                q_copy(f).start()

    lane = lax.broadcasted_iota(jnp.int32, (tok, PW), 1)

    def attend(q, p, slots):
        q32 = q.astype(F32)
        both = jnp.concatenate(
            [
                jnp.where((lane >= h * 64) & (lane < h * 64 + 64), q32, 0.0).astype(BF16)
                for h in range(2)
            ],
            axis=0,
        )
        top = jnp.full((1, 2 * tok), -jnp.inf, F32)
        for j, slot in enumerate(slots):
            sc = lax.dot_general(
                kv[0, p, slot], both, (((1,), (1,)), ((), ())), preferred_element_type=F32
            )
            sbuf[j] = sc
            top = jnp.maximum(top, jnp.max(sc, axis=0, keepdims=True))

        totals = [jnp.zeros((1, tok), F32)] * 2
        accs = [jnp.zeros((64, tok), F32)] * 2
        for j, slot in enumerate(slots):
            v = kv[1, p, slot].T
            for h in range(2):
                cols = slice(h * tok, h * tok + tok)
                wts = jnp.exp(sbuf[j, :, cols] - top[:, cols])
                totals[h] += jnp.sum(wts, axis=0, keepdims=True)
                accs[h] += jnp.dot(
                    v[h * 64 : h * 64 + 64, :], wts.astype(BF16), preferred_element_type=F32
                )
        return [(top[:, h * tok : h * tok + tok], totals[h], accs[h]) for h in range(2)]

    def step(p, _):
        cols = pl.ds(pl.multiple_of(p * PW, PW), PW)
        lent = is_lent(n, p)
        f = lent_index(p)

        pump(p + n - 1)

        serve = lent & is_server
        alone = lent & is_end

        @pl.when(serve)
        def _():
            for c in own_copies(p):
                c.start()

        for j in range(1, n):

            @pl.when(jnp.logical_not(alone | has_right) & (me - j >= 0))
            def _():
                for c in range(2):
                    kv_copy(p, me - j, c, True).wait_recv()

            @pl.when(jnp.logical_not(alone | has_left) & (me + j <= last))
            def _():
                for c in range(2):
                    kv_copy(p, me + j, c, False).wait_recv()

        if n >= 4:

            @pl.when(serve)
            def _():
                for c in own_copies(p):
                    c.wait()
                q_copy(f).wait_recv()

                def slot(j):
                    s = j + jnp.where(served == 0, 1, 0)
                    return jnp.where(s == me, n, s)

                for h, (top, total, acc) in enumerate(
                    attend(q_in[f], p, [slot(j) for j in range(n - 1)])
                ):
                    lent_out[f, h * 64 : h * 64 + 64, :] = (acc / total).astype(BF16)
                    stat_out[f, h : h + 1, :] = top
                    stat_out[f, 2 + h : 3 + h, :] = total
                stat_out[f, 4:8, :] = jnp.zeros((4, tok), F32)
                lent_copy(f).start()
                stat_copy(f).start()

        @pl.when(jnp.logical_not(alone))
        def _():
            for h, (top, total, acc) in enumerate(attend(q_ref[p], p, range(n))):
                ot[h * 64 : h * 64 + 64, :] = acc / total

        if n >= 4:

            @pl.when(alone)
            def _():
                mine = attend(q_ref[p], p, [me])
                lent_copy(f).wait_recv()
                stat_copy(f).wait_recv()
                for h, (top, total, acc) in enumerate(mine):
                    top_b = stat_in[f, h : h + 1, :]
                    total_b = stat_in[f, 2 + h : 3 + h, :]
                    high = jnp.maximum(top, top_b)
                    fac_a = jnp.exp(top - high)
                    fac_b = jnp.exp(top_b - high) * total_b
                    got = lent_in[f, h * 64 : h * 64 + 64, :].astype(F32)
                    ot[h * 64 : h * 64 + 64, :] = (acc * fac_a + got * fac_b) / (
                        total * fac_a + fac_b
                    )

        new = (hid[:, cols].astype(F32) + ot[...].T).astype(BF16)
        upd[:, cols] = new
        new32 = new.astype(F32)
        sums[0:1, cols] = jnp.sum(new32, axis=0, keepdims=True)
        sums[1:2, cols] = jnp.sum(new32 * new32, axis=0, keepdims=True)
        return 0

    lax.fori_loop(0, pairs, step, 0)

    factors(1, sums[0:1, :], sums[1:2, :], params[2:3, :], params[3:4, :])
    image_rows = tok // W

    def activate(i):
        x = upd[pl.ds(pl.multiple_of(i * W, W), W), :].astype(F32)
        v = x * rows_n[0:1, :] + rows_n[1:2, :]
        act[pl.ds(pl.multiple_of(i * W + W, W), W), :] = (v / (1.0 + jnp.exp(-v))).astype(BF16)

    activate(jnp.int32(0))
    activate(jnp.int32(image_rows - 1))
    up = remote(
        act.at[pl.ds(W, W)],
        act.at[pl.ds(tok + W, W)],
        halo_send.at[0],
        halo_recv.at[0],
        me - 1,
    )
    down = remote(
        act.at[pl.ds(tok, W)], act.at[pl.ds(0, W)], halo_send.at[1], halo_recv.at[1], me + 1
    )

    @pl.when(has_left)
    def _():
        up.start()

    @pl.when(has_right)
    def _():
        down.start()

    lax.fori_loop(1, image_rows - 1, lambda i, c: (activate(i), c)[1], 0)
    load_conv.wait()

    def middle_tap(b, _):
        ybuf[b] = jnp.dot(act[W : W + tok, :], wconv[3 + b], preferred_element_type=F32)
        return 0

    lax.fori_loop(0, 3, middle_tap, 0)

    @pl.when(has_right)
    def _():
        up.wait_recv()

    @pl.when(jnp.logical_not(has_right))
    def _():
        act[tok + W : tok + 2 * W, :] = jnp.zeros((W, chan), BF16)

    @pl.when(has_left)
    def _():
        down.wait_recv()

    @pl.when(jnp.logical_not(has_left))
    def _():
        act[0:W, :] = jnp.zeros((W, chan), BF16)

    def outer_tap(t, _):
        a, b = lax.div(t, 3) * 2, lax.rem(t, 3)
        rows = pl.ds(pl.multiple_of(a * W, W), tok)
        ybuf[b] += jnp.dot(act[rows, :], wconv[a * 3 + b], preferred_element_type=F32)
        return 0

    lax.fori_loop(0, 6, outer_tap, 0)

    cout = out_ref.shape[1]
    column = lax.rem(lax.broadcasted_iota(jnp.int32, (tok, cout), 0), W)
    before = jnp.where(column == 0, 0.0, pltpu.roll(ybuf[0], 1, 0))
    after = jnp.where(column == W - 1, 0.0, pltpu.roll(ybuf[2], tok - 1, 0))
    out_ref[...] = (before + ybuf[1] + after + params[4:5, 0:cout]).astype(BF16)

    def drain(p, _):
        for right in (True, False):
            for j in range(n):
                s = me - j if right else me + j
                ok = (s >= 0) if right else (s <= last)

                @pl.when(goes(right, p) & ok)
                def _():
                    for c in range(2):
                        kv_copy(p, s, c, right).wait_send()

        return 0

    lax.fori_loop(0, pairs, drain, 0)
    for j in range(n):

        @pl.when(has_right & (me - j >= 0))
        def _():
            mom_copy(me - j, True).wait_send()

        @pl.when(has_left & (me + j <= last))
        def _():
            mom_copy(me + j, False).wait_send()

    if n >= 4:

        @pl.when(is_end)
        def _():
            for f in range(n_lent):
                q_copy(f).wait_send()

        @pl.when(is_server)
        def _():
            for f in range(n_lent):
                lent_copy(f).wait_send()
                stat_copy(f).wait_send()

    @pl.when(has_left)
    def _():
        up.wait_send()

    @pl.when(has_right)
    def _():
        down.wait_send()


def time_embedding(timestep, w_time):
    half_dim = w_time.shape[0] // 2
    frequency = jnp.exp(-math.log(10000.0) * jnp.arange(half_dim, dtype=jnp.float32) / half_dim)
    angles = timestep[0].astype(jnp.float32) * frequency
    embedded = jnp.concatenate([jnp.cos(angles), jnp.sin(angles)])
    return jnp.dot(embedded[None, :], w_time.astype(jnp.float32), precision=lax.Precision.HIGHEST)


def body(
    n,
    hidden_in,
    stale_keys,
    stale_values,
    stale_moments,
    gain_attn,
    bias_attn,
    w_query,
    w_key,
    w_value,
    gain_conv,
    bias_conv,
    conv_weight,
    conv_bias,
    w_time,
    timestep,
):
    tok, chan = hidden_in.shape
    cout = conv_weight.shape[3]
    pairs = chan // PW
    lent = 4
    bias_out = time_embedding(timestep, w_time) + conv_bias[None, :]
    rows = [gain_attn, bias_attn, gain_conv, bias_conv, jnp.pad(bias_out[0], (0, chan - cout))]
    params = jnp.stack(rows + [jnp.zeros((chan,), F32)] * 3)
    vmem = pl.BlockSpec(memory_space=pltpu.VMEM)
    hbm = pl.BlockSpec(memory_space=pl.ANY)
    dma = pltpu.SemaphoreType.DMA
    return pl.pallas_call(
        functools.partial(kernel, n),
        out_shape=jax.ShapeDtypeStruct((tok, cout), BF16),
        in_specs=[hbm] * 4 + [vmem] + [hbm] * 4,
        out_specs=vmem,
        scratch_shapes=[
            pltpu.VMEM((tok, chan), BF16),
            pltpu.VMEM((3, chan, chan), BF16),
            pltpu.VMEM((9, chan, cout), BF16),
            pltpu.VMEM((2, pairs, n + 1, tok, PW), BF16),
            pltpu.VMEM((pairs, tok, PW), BF16),
            pltpu.VMEM((lent, tok, PW), BF16),
            pltpu.VMEM((lent, PW, tok), BF16),
            pltpu.VMEM((lent, PW, tok), BF16),
            pltpu.VMEM((lent, 8, tok), F32),
            pltpu.VMEM((lent, 8, tok), F32),
            pltpu.VMEM((n, tok, 2 * tok), F32),
            pltpu.VMEM((PW, tok), F32),
            pltpu.VMEM((tok, chan), BF16),
            pltpu.VMEM((tok + 2 * W, chan), BF16),
            pltpu.VMEM((3, tok, cout), F32),
            pltpu.VMEM((8, chan), F32),
            pltpu.VMEM((8, chan), F32),
            pltpu.VMEM((n, 8, 128), F32),
            pltpu.VMEM(stale_moments.shape, F32),
            dma((8,)),
            dma((pairs, n, 2)),
            dma((pairs, n, 2)),
            dma((pairs, n, 2)),
            dma((n, 2)),
            dma((n,)),
            dma((3, lent)),
            dma((3, lent)),
            dma((2,)),
            dma((2,)),
        ],
        compiler_params=pltpu.CompilerParams(
            collective_id=0,
            has_side_effects=True,
            vmem_limit_bytes=63 * 1024 * 1024,
        ),
        cost_estimate=pl.CostEstimate(
            flops=2 * tok * chan * (3 * chan + 2 * n * tok + 9 * cout),
            bytes_accessed=2 * (3 * chan * chan + 9 * chan * cout + 4 * tok * chan),
            transcendentals=HEADS * n * tok * tok,
        ),
    )(
        hidden_in,
        stale_keys,
        stale_values,
        stale_moments,
        params,
        w_query,
        w_key,
        w_value,
        conv_weight.reshape(9, chan, cout),
    )


def solution(mesh):
    split = P(("batch", "patch"), None)
    return jax.shard_map(
        functools.partial(body, mesh.shape["patch"]),
        mesh=mesh,
        in_specs=(split, split, split, P(("batch", "patch"), None, None, None)) + (P(),) * 11,
        out_specs=split,
        check_vma=False,
    )
```

```python
import functools
import math

import jax
import jax.numpy as jnp
from jax import lax
from jax.experimental import pallas as pl
from jax.experimental.pallas import tpu as pltpu
from jax.sharding import PartitionSpec as P

HEADS = 20
GROUPS = 32
W = 64
EPS = 1e-05
PW = 128
F32 = jnp.float32
BF16 = jnp.bfloat16
HI = lax.Precision.HIGHEST


def is_lent(n, p):
    if n < 4:
        return p < 0
    return (lax.rem(p, 2) == 0) & (p >= 2)


def lent_index(p):
    return jnp.maximum(lax.div(p, 2) - 1, 0)


def kernel(
    n,
    hidden_hbm,
    keys_hbm,
    values_hbm,
    moments_hbm,
    params,
    wqkv_q,
    wqkv_k,
    wqkv_v,
    wconv_hbm,
    out_ref,
    hid,
    wq,
    wconv,
    kv,
    q_ref,
    q_in,
    lent_out,
    lent_in,
    stat_out,
    stat_in,
    sbuf,
    ot,
    upd,
    act,
    ybuf,
    sums,
    rows_n,
    mom,
    mom_own,
    local_sem,
    send_r,
    send_l,
    recv,
    mom_send,
    mom_recv,
    lend_send,
    lend_recv,
    halo_send,
    halo_recv,
):
    me = lax.axis_index("patch")
    tok, chan = hid.shape
    pairs = chan // PW
    count = n * tok * (chan // GROUPS)
    last = n - 1
    has_left, has_right = me > 0, me < last
    is_end = (me == 0) | (me == last)
    is_server = ((me == 1) | (me == n - 2)) if n >= 4 else (me < 0)
    served = jnp.where(me == 1, 0, last)
    server = jnp.where(me == 0, 1, last - 1)

    def remote(src, dst, ssem, rsem, to):
        return pltpu.make_async_remote_copy(
            src_ref=src,
            dst_ref=dst,
            send_sem=ssem,
            recv_sem=rsem,
            device_id={"patch": to},
            device_id_type=pl.DeviceIdType.MESH,
        )

    barrier = pltpu.get_barrier_semaphore()

    @pl.when(has_left)
    def _():
        pl.semaphore_signal(
            barrier, inc=1, device_id={"patch": me - 1}, device_id_type=pl.DeviceIdType.MESH
        )

    @pl.when(has_right)
    def _():
        pl.semaphore_signal(
            barrier, inc=1, device_id={"patch": me + 1}, device_id_type=pl.DeviceIdType.MESH
        )

    load_hid = pltpu.make_async_copy(hidden_hbm, hid, local_sem.at[0])
    load_hid.start()
    load_mom = pltpu.make_async_copy(moments_hbm, mom_own, local_sem.at[7])
    load_mom.start()
    load_w = [
        pltpu.make_async_copy(w, wq.at[i], local_sem.at[1 + i])
        for i, w in enumerate((wqkv_q, wqkv_k, wqkv_v))
    ]
    for c in load_w:
        c.start()

    load_mom.wait()
    own4 = jnp.sum(mom_own[...], axis=0)
    own_row = jnp.concatenate(
        [own4[i, k : k + 1, :] for i in range(2) for k in range(2)], axis=1
    )
    mom[me] = jnp.broadcast_to(own_row, (8, 128))

    pl.semaphore_wait(barrier, has_left.astype(jnp.int32) + has_right.astype(jnp.int32))

    def mom_copy(s, right):
        return remote(
            mom.at[s],
            mom.at[s],
            mom_send.at[s, 1 if right else 0],
            mom_recv.at[s],
            me + 1 if right else me - 1,
        )

    @pl.when(has_right)
    def _():
        mom_copy(me, True).start()

    @pl.when(has_left)
    def _():
        mom_copy(me, False).start()

    def goes(right, p):
        if right:
            return has_right & jnp.logical_not(is_lent(n, p) & (me + 1 == last))
        return has_left & jnp.logical_not(is_lent(n, p) & (me - 1 == 0))

    def kv_copy(p, s, c, right, src=None):
        dst = kv.at[c, p, s]
        return remote(
            dst if src is None else src,
            dst,
            (send_r if right else send_l).at[p, s, c],
            recv.at[p, s, c],
            me + 1 if right else me - 1,
        )

    def send_own(p):
        cols = pl.ds(pl.multiple_of(p * PW, PW), PW)
        for right in (True, False):

            @pl.when(goes(right, p))
            def _():
                for c, ref in enumerate((keys_hbm, values_hbm)):
                    kv_copy(p, me, c, right, ref.at[:, cols]).start()

    def forward(p, j):
        @pl.when(has_right & (me - j >= 0))
        def _():
            for c in range(2):
                kv_copy(p, me - j, c, True).wait_recv()

                @pl.when(goes(True, p))
                def _():
                    kv_copy(p, me - j, c, True).start()

        @pl.when(has_left & (me + j <= last))
        def _():
            for c in range(2):
                kv_copy(p, me + j, c, False).wait_recv()

                @pl.when(goes(False, p))
                def _():
                    kv_copy(p, me + j, c, False).start()

    def pump(t):
        @pl.when(t + 1 < pairs)
        def _():
            send_own(t + 1)

        for j in range(1, n - 1):

            @pl.when((t - j >= 0) & (t - j < pairs))
            def _():
                forward(t - j, j)

    send_own(jnp.int32(0))
    send_own(jnp.int32(1))
    send_own(jnp.int32(2))

    load_conv = pltpu.make_async_copy(wconv_hbm, wconv, local_sem.at[4])
    load_conv.start()

    def own_copies(p):
        cols = pl.ds(pl.multiple_of(p * PW, PW), PW)
        return [
            pltpu.make_async_copy(ref.at[:, cols], kv.at[c, p, n], local_sem.at[5 + c])
            for c, ref in enumerate((keys_hbm, values_hbm))
        ]

    load_hid.wait()

    def column_sums(i, carry):
        a, b = carry
        x = hid[pl.ds(pl.multiple_of(i * W, W), W), :].astype(F32)
        return (
            a + jnp.sum(x, axis=0, keepdims=True),
            b + jnp.sum(x * x, axis=0, keepdims=True),
        )

    zero_row = jnp.zeros((1, chan), F32)
    sum_x, sum_xx = lax.fori_loop(0, tok // W, column_sums, (zero_row, zero_row))

    for j in range(1, n):

        @pl.when(me - j >= 0)
        def _():
            mom_copy(me - j, True).wait_recv()

            @pl.when(has_right)
            def _():
                mom_copy(me - j, True).start()

        @pl.when(me + j <= last)
        def _():
            mom_copy(me + j, False).wait_recv()

            @pl.when(has_left)
            def _():
                mom_copy(me + j, False).start()

    def others(s, row):
        return row + jnp.where(s == me, 0.0, mom[s])

    other_rows = lax.fori_loop(0, n, others, jnp.zeros((8, 128), F32))
    mom_total = jnp.broadcast_to(other_rows[0:1], (8, 128))

    group_of = lax.div(lax.broadcasted_iota(jnp.int32, (chan, 128), 0), chan // GROUPS)
    lane_of = lax.broadcasted_iota(jnp.int32, (chan, 128), 1)

    def spread(k):
        return (lane_of == group_of + k * GROUPS).astype(F32)

    def factors(norm, s_x, s_xx, gain, offset):
        e_sum, e_sq = spread(2 * norm), spread(2 * norm + 1)
        own = jnp.dot(
            jnp.broadcast_to(s_x, (8, chan)), e_sum, precision=HI, preferred_element_type=F32
        ) + jnp.dot(
            jnp.broadcast_to(s_xx, (8, chan)), e_sq, precision=HI, preferred_element_type=F32
        )
        totals = mom_total + own
        nt = (((1,), (1,)), ((), ()))
        first = lax.dot_general(totals, e_sum, nt, precision=HI, preferred_element_type=F32)
        second = lax.dot_general(totals, e_sq, nt, precision=HI, preferred_element_type=F32)
        average = first[0:1] / count
        variance = second[0:1] / count - average * average
        inverse = lax.rsqrt(variance + EPS)
        rows_n[0:1, :] = inverse * gain
        rows_n[1:2, :] = offset - average * inverse * gain

    factors(0, sum_x, sum_xx, params[0:1, :], params[1:2, :])

    def normalize(i, _):
        rows = pl.ds(pl.multiple_of(i * W, W), W)
        upd[rows, :] = (hid[rows, :].astype(F32) * rows_n[0:1, :] + rows_n[1:2, :]).astype(BF16)
        return 0

    lax.fori_loop(0, tok // W, normalize, 0)
    for c in load_w:
        c.wait()
    for j in range(1, n - 1):
        if j < 2:
            forward(jnp.int32(0), j)
    scale = (chan // HEADS) ** (-0.5)

    def project(j, _):
        @pl.when(j == 2)
        def _():
            for t in range(2, n - 1):
                pump(jnp.int32(t))

        cols = pl.ds(pl.multiple_of(j * 2 * PW, 2 * PW), 2 * PW)
        for i in range(3):
            r = jnp.dot(upd[...], wq[i, :, cols], preferred_element_type=F32).astype(BF16)
            for half in range(2):
                piece = r[:, half * PW : (half + 1) * PW]
                if i == 0:
                    q_ref[2 * j + half] = (piece.astype(F32) * scale).astype(BF16)
                else:
                    kv[i - 1, 2 * j + half, me] = piece
        return 0

    lax.fori_loop(0, chan // (2 * PW), project, 0)

    def q_copy(f):
        return remote(
            q_ref.at[2 * f + 2], q_in.at[f], lend_send.at[0, f], lend_recv.at[0, f], server
        )

    def lent_copy(f):
        return remote(
            lent_out.at[f], lent_in.at[f], lend_send.at[1, f], lend_recv.at[1, f], served
        )

    def stat_copy(f):
        return remote(
            stat_out.at[f], stat_in.at[f], lend_send.at[2, f], lend_recv.at[2, f], served
        )

    n_lent = q_in.shape[0]
    if n >= 4:

        @pl.when(is_end)
        def _():
            for f in range(n_lent):
                q_copy(f).start()

    lane = lax.broadcasted_iota(jnp.int32, (tok, PW), 1)

    def attend(q, p, slots):
        q32 = q.astype(F32)
        both = jnp.concatenate(
            [
                jnp.where((lane >= h * 64) & (lane < h * 64 + 64), q32, 0.0).astype(BF16)
                for h in range(2)
            ],
            axis=0,
        )
        top = jnp.full((1, 2 * tok), -jnp.inf, F32)
        for j, slot in enumerate(slots):
            sc = lax.dot_general(
                kv[0, p, slot], both, (((1,), (1,)), ((), ())), preferred_element_type=F32
            )
            sbuf[j] = sc
            top = jnp.maximum(top, jnp.max(sc, axis=0, keepdims=True))

        totals = [jnp.zeros((1, tok), F32)] * 2
        accs = [jnp.zeros((64, tok), F32)] * 2
        for j, slot in enumerate(slots):
            v = kv[1, p, slot].T
            for h in range(2):
                cols = slice(h * tok, h * tok + tok)
                wts = jnp.exp(sbuf[j, :, cols] - top[:, cols])
                totals[h] += jnp.sum(wts, axis=0, keepdims=True)
                accs[h] += jnp.dot(
                    v[h * 64 : h * 64 + 64, :], wts.astype(BF16), preferred_element_type=F32
                )
        return [(top[:, h * tok : h * tok + tok], totals[h], accs[h]) for h in range(2)]

    def step(p, _):
        cols = pl.ds(pl.multiple_of(p * PW, PW), PW)
        lent = is_lent(n, p)
        f = lent_index(p)

        pump(p + n - 1)

        serve = lent & is_server
        alone = lent & is_end

        @pl.when(serve)
        def _():
            for c in own_copies(p):
                c.start()

        for j in range(1, n):

            @pl.when(jnp.logical_not(alone | has_right) & (me - j >= 0))
            def _():
                for c in range(2):
                    kv_copy(p, me - j, c, True).wait_recv()

            @pl.when(jnp.logical_not(alone | has_left) & (me + j <= last))
            def _():
                for c in range(2):
                    kv_copy(p, me + j, c, False).wait_recv()

        if n >= 4:

            @pl.when(serve)
            def _():
                for c in own_copies(p):
                    c.wait()
                q_copy(f).wait_recv()

                def slot(j):
                    s = j + jnp.where(served == 0, 1, 0)
                    return jnp.where(s == me, n, s)

                for h, (top, total, acc) in enumerate(
                    attend(q_in[f], p, [slot(j) for j in range(n - 1)])
                ):
                    lent_out[f, h * 64 : h * 64 + 64, :] = (acc / total).astype(BF16)
                    stat_out[f, h : h + 1, :] = top
                    stat_out[f, 2 + h : 3 + h, :] = total
                stat_out[f, 4:8, :] = jnp.zeros((4, tok), F32)
                lent_copy(f).start()
                stat_copy(f).start()

        @pl.when(jnp.logical_not(alone))
        def _():
            for h, (top, total, acc) in enumerate(attend(q_ref[p], p, range(n))):
                ot[h * 64 : h * 64 + 64, :] = acc / total

        if n >= 4:

            @pl.when(alone)
            def _():
                mine = attend(q_ref[p], p, [me])
                lent_copy(f).wait_recv()
                stat_copy(f).wait_recv()
                for h, (top, total, acc) in enumerate(mine):
                    top_b = stat_in[f, h : h + 1, :]
                    total_b = stat_in[f, 2 + h : 3 + h, :]
                    high = jnp.maximum(top, top_b)
                    fac_a = jnp.exp(top - high)
                    fac_b = jnp.exp(top_b - high) * total_b
                    got = lent_in[f, h * 64 : h * 64 + 64, :].astype(F32)
                    ot[h * 64 : h * 64 + 64, :] = (acc * fac_a + got * fac_b) / (
                        total * fac_a + fac_b
                    )

        new = (hid[:, cols].astype(F32) + ot[...].T).astype(BF16)
        upd[:, cols] = new
        new32 = new.astype(F32)
        sums[0:1, cols] = jnp.sum(new32, axis=0, keepdims=True)
        sums[1:2, cols] = jnp.sum(new32 * new32, axis=0, keepdims=True)
        return 0

    lax.fori_loop(0, pairs, step, 0)

    factors(1, sums[0:1, :], sums[1:2, :], params[2:3, :], params[3:4, :])
    image_rows = tok // W

    def activate(i):
        x = upd[pl.ds(pl.multiple_of(i * W, W), W), :].astype(F32)
        v = x * rows_n[0:1, :] + rows_n[1:2, :]
        act[pl.ds(pl.multiple_of(i * W + W, W), W), :] = (v / (1.0 + jnp.exp(-v))).astype(BF16)

    activate(jnp.int32(0))
    activate(jnp.int32(image_rows - 1))
    up = remote(
        act.at[pl.ds(W, W)],
        act.at[pl.ds(tok + W, W)],
        halo_send.at[0],
        halo_recv.at[0],
        me - 1,
    )
    down = remote(
        act.at[pl.ds(tok, W)], act.at[pl.ds(0, W)], halo_send.at[1], halo_recv.at[1], me + 1
    )

    @pl.when(has_left)
    def _():
        up.start()

    @pl.when(has_right)
    def _():
        down.start()

    lax.fori_loop(1, image_rows - 1, lambda i, c: (activate(i), c)[1], 0)
    load_conv.wait()

    def middle_tap(b, _):
        ybuf[b] = jnp.dot(act[W : W + tok, :], wconv[3 + b], preferred_element_type=F32)
        return 0

    lax.fori_loop(0, 3, middle_tap, 0)

    @pl.when(has_right)
    def _():
        up.wait_recv()

    @pl.when(jnp.logical_not(has_right))
    def _():
        act[tok + W : tok + 2 * W, :] = jnp.zeros((W, chan), BF16)

    @pl.when(has_left)
    def _():
        down.wait_recv()

    @pl.when(jnp.logical_not(has_left))
    def _():
        act[0:W, :] = jnp.zeros((W, chan), BF16)

    def outer_tap(t, _):
        a, b = lax.div(t, 3) * 2, lax.rem(t, 3)
        rows = pl.ds(pl.multiple_of(a * W, W), tok)
        ybuf[b] += jnp.dot(act[rows, :], wconv[a * 3 + b], preferred_element_type=F32)
        return 0

    lax.fori_loop(0, 6, outer_tap, 0)

    cout = out_ref.shape[1]
    column = lax.rem(lax.broadcasted_iota(jnp.int32, (tok, cout), 0), W)
    before = jnp.where(column == 0, 0.0, pltpu.roll(ybuf[0], 1, 0))
    after = jnp.where(column == W - 1, 0.0, pltpu.roll(ybuf[2], tok - 1, 0))
    out_ref[...] = (before + ybuf[1] + after + params[4:5, 0:cout]).astype(BF16)

    def drain(p, _):
        for right in (True, False):
            for j in range(n):
                s = me - j if right else me + j
                ok = (s >= 0) if right else (s <= last)

                @pl.when(goes(right, p) & ok)
                def _():
                    for c in range(2):
                        kv_copy(p, s, c, right).wait_send()

        return 0

    lax.fori_loop(0, pairs, drain, 0)
    for j in range(n):

        @pl.when(has_right & (me - j >= 0))
        def _():
            mom_copy(me - j, True).wait_send()

        @pl.when(has_left & (me + j <= last))
        def _():
            mom_copy(me + j, False).wait_send()

    if n >= 4:

        @pl.when(is_end)
        def _():
            for f in range(n_lent):
                q_copy(f).wait_send()

        @pl.when(is_server)
        def _():
            for f in range(n_lent):
                lent_copy(f).wait_send()
                stat_copy(f).wait_send()

    @pl.when(has_left)
    def _():
        up.wait_send()

    @pl.when(has_right)
    def _():
        down.wait_send()


def time_embedding(timestep, w_time):
    half_dim = w_time.shape[0] // 2
    frequency = jnp.exp(-math.log(10000.0) * jnp.arange(half_dim, dtype=jnp.float32) / half_dim)
    angles = timestep[0].astype(jnp.float32) * frequency
    embedded = jnp.concatenate([jnp.cos(angles), jnp.sin(angles)])
    return jnp.dot(embedded[None, :], w_time.astype(jnp.float32), precision=lax.Precision.HIGHEST)


def body(
    n,
    hidden_in,
    stale_keys,
    stale_values,
    stale_moments,
    gain_attn,
    bias_attn,
    w_query,
    w_key,
    w_value,
    gain_conv,
    bias_conv,
    conv_weight,
    conv_bias,
    w_time,
    timestep,
):
    tok, chan = hidden_in.shape
    cout = conv_weight.shape[3]
    pairs = chan // PW
    lent = 4
    bias_out = time_embedding(timestep, w_time) + conv_bias[None, :]
    rows = [gain_attn, bias_attn, gain_conv, bias_conv, jnp.pad(bias_out[0], (0, chan - cout))]
    params = jnp.stack(rows + [jnp.zeros((chan,), F32)] * 3)
    vmem = pl.BlockSpec(memory_space=pltpu.VMEM)
    hbm = pl.BlockSpec(memory_space=pl.ANY)
    dma = pltpu.SemaphoreType.DMA
    return pl.pallas_call(
        functools.partial(kernel, n),
        out_shape=jax.ShapeDtypeStruct((tok, cout), BF16),
        in_specs=[hbm] * 4 + [vmem] + [hbm] * 4,
        out_specs=vmem,
        scratch_shapes=[
            pltpu.VMEM((tok, chan), BF16),
            pltpu.VMEM((3, chan, chan), BF16),
            pltpu.VMEM((9, chan, cout), BF16),
            pltpu.VMEM((2, pairs, n + 1, tok, PW), BF16),
            pltpu.VMEM((pairs, tok, PW), BF16),
            pltpu.VMEM((lent, tok, PW), BF16),
            pltpu.VMEM((lent, PW, tok), BF16),
            pltpu.VMEM((lent, PW, tok), BF16),
            pltpu.VMEM((lent, 8, tok), F32),
            pltpu.VMEM((lent, 8, tok), F32),
            pltpu.VMEM((n, tok, 2 * tok), F32),
            pltpu.VMEM((PW, tok), F32),
            pltpu.VMEM((tok, chan), BF16),
            pltpu.VMEM((tok + 2 * W, chan), BF16),
            pltpu.VMEM((3, tok, cout), F32),
            pltpu.VMEM((8, chan), F32),
            pltpu.VMEM((8, chan), F32),
            pltpu.VMEM((n, 8, 128), F32),
            pltpu.VMEM(stale_moments.shape, F32),
            dma((8,)),
            dma((pairs, n, 2)),
            dma((pairs, n, 2)),
            dma((pairs, n, 2)),
            dma((n, 2)),
            dma((n,)),
            dma((3, lent)),
            dma((3, lent)),
            dma((2,)),
            dma((2,)),
        ],
        compiler_params=pltpu.CompilerParams(
            collective_id=0,
            has_side_effects=True,
            vmem_limit_bytes=63 * 1024 * 1024,
        ),
        cost_estimate=pl.CostEstimate(
            flops=2 * tok * chan * (3 * chan + 2 * n * tok + 9 * cout),
            bytes_accessed=2 * (3 * chan * chan + 9 * chan * cout + 4 * tok * chan),
            transcendentals=HEADS * n * tok * tok,
        ),
    )(
        hidden_in,
        stale_keys,
        stale_values,
        stale_moments,
        params,
        w_query,
        w_key,
        w_value,
        conv_weight.reshape(9, chan, cout),
    )


def solution(mesh):
    split = P(("batch", "patch"), None)
    return jax.shard_map(
        functools.partial(body, mesh.shape["patch"]),
        mesh=mesh,
        in_specs=(split, split, split, P(("batch", "patch"), None, None, None)) + (P(),) * 11,
        out_specs=split,
        check_vma=False,
    )
```
